32 devices in a mesh: tok: 8 (over z, y), wid: 4 (over x, core).
Axes of the slice: x: 2, y: 2, z: 4, core: 2. Of those that a mesh axis runs over, the one named last changes fastest.
Arguments:
- queries: bfloat16 [1024, 8192], P('tok', 'wid'), may hold values from -6 to 6
- key_branch: bfloat16 [1024, 8192], P('tok', 'wid'), may hold values from -6 to 6
- value_branch: bfloat16 [1024, 8192], P('tok', 'wid'), may hold values from -6 to 6
- filters: float32 [512, 128], P('wid'), may hold values from -0.5 to 0.5
- out_weight: bfloat16 [8192, 8192], P(None, 'wid'), may hold values from -0.09375 to 0.09375
- cotangent: bfloat16 [1024, 8192], P('tok', 'wid'), may hold values from -6 to 6
Outputs:
- layer_out: bfloat16 [1024, 8192], P('tok', 'wid')
- grad_queries: bfloat16 [1024, 8192], P('tok', 'wid')
- grad_keys: bfloat16 [1024, 8192], P('tok', 'wid')
- grad_values: bfloat16 [1024, 8192], P('tok', 'wid')
- grad_filters: float32 [512, 128], P('wid')
The draws below stay inside these ranges and needn't reach their ends.
All inputs are finite; a program needn't handle non-finite values.
Results may differ from the reference program's by a relative error of at most 0.02.
Values may be sent and summed in bfloat16 or wider, within the bound.
A program may use at most 192 MiB of HBM per device.

```python
import math
import jax
import jax.numpy as jnp
from jax import lax

D = 8192
KERNEL = 128
GROUP = 16
TOKENS = 1024
FILTERS = 512
N_WID = 4


def with_spikes(array, stream_key, source, target, shards_of, factor):
    def block_of(position):
        return (jnp.arange(array.shape[position]) // (array.shape[position] // shards_of)).reshape((-1,) + (1,) * (array.ndim - 1 - position))

    one_side = jax.random.permutation(stream_key, shards_of)[block_of(target)]
    second = (block_of(target) + shards_of // 2) % shards_of
    return jnp.where((block_of(source) == one_side) | (block_of(source) == second), factor * array, array)


def level_of(key, shape, pieces, low, high):
    gain, own = 1.0, jax.random.fold_in(key, 6)
    for dim, blocks in pieces:
        heights = jnp.exp(jax.random.uniform(jax.random.fold_in(own, dim), (blocks,), jnp.float32, low / len(pieces), high / len(pieces)))
        gain = gain * jnp.repeat(heights, shape[dim] // blocks).reshape([-1 if axis == dim else 1 for axis in range(len(shape))])
    return gain


def bell_draw(rng, shape, scale, reach, pieces=(), held_as=jnp.bfloat16):
    result = scale * jax.random.normal(rng, shape, jnp.float32)
    if pieces:
        result = result * level_of(rng, shape, pieces, -0.22, 0.18)
    return jnp.clip(result, -reach, reach).astype(held_as)


def noise_with(rng, shape, scale, limit, shards, heavy, kind=jnp.bfloat16):
    values = scale * jax.random.normal(rng, shape, jnp.float32)
    if shards:
        values = values * level_of(rng, shape, shards, -0.22, 0.18)
    return jnp.clip(with_spikes(values, jax.random.fold_in(rng, 3), *heavy), -limit, limit).astype(kind)


def setup_inputs(seed: int = 0) -> dict:
    seeds = jax.random.split(jax.random.key(seed), 7)
    return {
        "queries": bell_draw(seeds[0], (TOKENS, D), 1.0, 6.0, ((0, 8), (1, 4))),
        "key_branch": bell_draw(seeds[1], (TOKENS, D), 1.0, 6.0, ((0, 8), (1, 4))),
        "value_branch": bell_draw(seeds[2], (TOKENS, D), 1.0, 6.0, ((0, 8), (1, 4))),
        "filters": bell_draw(seeds[3], (FILTERS, KERNEL), KERNEL ** -0.5, 0.5, ((0, 4),), jnp.float32),
        "out_weight": noise_with(seeds[4], (D, D), D ** -0.5, 0.09375, ((1, 4),), (1, 0, 4, 2.0)),
        "cotangent": bell_draw(seeds[5], (TOKENS, D), 1.0, 6.0, ((0, 8), (1, 4))),
    }


def reference(queries, key_branch, value_branch, filters, out_weight, cotangent):
    kv = (key_branch.astype(jnp.float32) * value_branch.astype(jnp.float32)).astype(jnp.bfloat16)
    kv_float = kv.astype(jnp.float32)
    chan_filters = jnp.repeat(filters, GROUP, axis=0)
    padded = jnp.concatenate([jnp.zeros((KERNEL, D), jnp.float32), kv_float], axis=0)

    def conv_tap(j, total):
        start = (KERNEL - j).astype(jnp.int32)
        shifted = lax.dynamic_slice_in_dim(padded, start, TOKENS, 0)
        taps = lax.dynamic_index_in_dim(chan_filters, j.astype(jnp.int32), 1, keepdims=False)
        return total + shifted * taps
    conv = lax.fori_loop(0, KERNEL, conv_tap, jnp.zeros((TOKENS, D), jnp.float32))
    gated = (queries.astype(jnp.float32) * conv).astype(jnp.bfloat16)
    layer_out = jnp.dot(gated, out_weight, preferred_element_type=jnp.float32).astype(jnp.bfloat16)
    block_width = D // N_WID

    def grad_block(n, total):
        start = (n * block_width).astype(jnp.int32)
        cot_block = lax.dynamic_slice_in_dim(cotangent, start, block_width, 1)
        weight_block = lax.dynamic_slice_in_dim(out_weight, start, block_width, 1)
        part = lax.dot_general(cot_block, weight_block, (((1,), (1,)), ((), ())), preferred_element_type=jnp.float32)
        rounded = lax.optimization_barrier(part.astype(jnp.bfloat16))
        return total + rounded.astype(jnp.float32)
    grad_gated = lax.fori_loop(0, N_WID, grad_block, jnp.zeros((TOKENS, D), jnp.float32))
    grad_conv = (grad_gated * queries.astype(jnp.float32)).astype(jnp.bfloat16)
    grad_queries = (grad_gated * conv).astype(jnp.bfloat16)
    grad_float = grad_conv.astype(jnp.float32)
    grad_padded = jnp.concatenate([grad_float, jnp.zeros((KERNEL, D), jnp.float32)], axis=0)

    def back_tap(j, total):
        shifted = lax.dynamic_slice_in_dim(grad_padded, j.astype(jnp.int32), TOKENS, 0)
        taps = lax.dynamic_index_in_dim(chan_filters, j.astype(jnp.int32), 1, keepdims=False)
        return total + shifted * taps
    grad_kv = lax.fori_loop(0, KERNEL, back_tap, jnp.zeros((TOKENS, D), jnp.float32))
    grad_keys = (grad_kv * value_branch.astype(jnp.float32)).astype(jnp.bfloat16)
    grad_values = (grad_kv * key_branch.astype(jnp.float32)).astype(jnp.bfloat16)

    def filter_tap(j):
        start = (KERNEL - j).astype(jnp.int32)
        shifted = lax.dynamic_slice_in_dim(padded, start, TOKENS, 0)
        return lax.optimization_barrier(jnp.sum(grad_float * shifted, axis=0))
    per_tap = lax.map(filter_tap, jnp.arange(KERNEL, dtype=jnp.int32))
    grouped = per_tap.T.reshape(FILTERS, GROUP, KERNEL).sum(axis=1)
    grad_filters = grouped * (1.0 / math.sqrt(TOKENS * GROUP))
    return (layer_out, grad_queries, grad_keys, grad_values, grad_filters)
```

```python
import functools
import math

import jax
import jax.numpy as jnp
from jax import lax
from jax.experimental import pallas as pl
from jax.experimental.pallas import tpu as pltpu
from jax.sharding import PartitionSpec as P


def shifted(block, axis, distance):
    devices = range(lax.axis_size(axis))
    route = [(i - distance, i) for i in devices if i - distance in devices]
    return lax.ppermute(block, axis, route)


def iota(shape, dim):
    return lax.broadcasted_iota(jnp.int32, shape, dim)


def circulant(row, kernel):
    return pltpu.roll(jnp.broadcast_to(row, (kernel, kernel)), 0, 1, stride=1, stride_axis=0)


def forward_tile(filters_rev, extended, group_size):
    groups, kernel = filters_rev.shape
    tile = extended.shape[1]
    row, lane = iota((kernel, kernel), 0), iota((kernel, kernel), 1)
    now = lane <= row
    owner = iota((kernel, tile), 1) // group_size
    result = jnp.zeros((kernel, tile), jnp.float32)
    for g in range(groups):
        ring = circulant(filters_rev[g : g + 1], kernel)
        both = jnp.concatenate(
            [jnp.where(now, 0.0, ring).astype(jnp.bfloat16), jnp.where(now, ring, 0.0).astype(jnp.bfloat16)],
            axis=1,
        )
        part = jnp.dot(both, extended, preferred_element_type=jnp.float32)
        result = jnp.where(owner == g, part, result)
    return result


def backward_tile(filters, grads, group_size):
    groups, kernel = filters.shape
    tile = grads.shape[1]
    row, lane = iota((kernel, kernel), 0), iota((kernel, kernel), 1)
    now = row <= lane
    owner = iota((kernel, tile), 1) // group_size
    result = jnp.zeros((kernel, tile), jnp.float32)
    for g in range(groups):
        ring = circulant(filters[g : g + 1], kernel)
        both = jnp.concatenate(
            [jnp.where(now, ring, 0.0).astype(jnp.bfloat16), jnp.where(now, 0.0, ring).astype(jnp.bfloat16)],
            axis=1,
        )
        part = jnp.dot(both, grads, preferred_element_type=jnp.float32)
        result = jnp.where(owner == g, part, result)
    return result


def filter_tile(extended, own_grads, groups, group_size):
    kernel, tile = own_grads.shape
    row, lane = iota((kernel, kernel), 0), iota((kernel, kernel), 1)
    now = row + lane >= kernel - 1
    owner = iota((2 * kernel, tile), 1) // group_size
    mirror = jnp.where(row + lane == kernel - 1, 1.0, 0.0).astype(jnp.bfloat16)
    extended = jnp.concatenate(
        [
            jnp.dot(mirror, half, preferred_element_type=jnp.float32).astype(jnp.bfloat16)
            for half in (extended[:kernel], extended[kernel:])
        ],
        axis=0,
    )
    rows = []
    for g in range(groups):
        part = lax.dot_general(
            jnp.where(owner == g, extended, jnp.zeros_like(extended)),
            own_grads,
            (((1,), (1,)), ((), ())),
            preferred_element_type=jnp.float32,
        )
        square = jnp.where(now, part[kernel:], part[:kernel])
        aligned = pltpu.roll(square, 1, 1, stride=1, stride_axis=0)
        rows.append(jnp.sum(aligned, axis=0, keepdims=True))
    return jnp.concatenate(rows, axis=0)


def forward_kernel(group_size, q_ref, kv_ref, rim_ref, filters_rev_ref, conv_ref, gated_ref):
    extended = jnp.concatenate([rim_ref[...], kv_ref[...]], axis=0)
    conv = forward_tile(filters_rev_ref[...], extended, group_size)
    conv_ref[...] = conv
    gated_ref[...] = (q_ref[...].astype(jnp.float32) * conv).astype(jnp.bfloat16)


def backward_kernel(
    group_size, k_ref, v_ref, rim_ref, gc_ref, gc_next_ref, filters_ref, gk_ref, gv_ref, gf_ref
):
    key, value = k_ref[...].astype(jnp.float32), v_ref[...].astype(jnp.float32)
    kv = (key * value).astype(jnp.bfloat16)
    extended = jnp.concatenate([rim_ref[...], kv], axis=0)
    own = gc_ref[...]
    filters = filters_ref[...]
    grad_kv = backward_tile(filters, jnp.concatenate([own, gc_next_ref[...]], axis=0), group_size)
    gk_ref[...] = (grad_kv * value).astype(jnp.bfloat16)
    gv_ref[...] = (grad_kv * key).astype(jnp.bfloat16)
    gf_ref[...] = filter_tile(extended, own, filters.shape[0], group_size)


def local(queries, key_branch, value_branch, filters, out_weight, cotangent):
    length, width = queries.shape
    groups, kernel = filters.shape
    group_size = width // groups
    tile = min(256, width)
    tile_groups = tile // group_size
    channels = pl.BlockSpec((length, tile), lambda i: (0, i))
    by_group = pl.BlockSpec((tile_groups, kernel), lambda i: (i, 0))
    wide = jax.ShapeDtypeStruct((length, width), jnp.bfloat16)
    flops = 2 * width * tile_groups * kernel * 2 * kernel

    kv = (key_branch.astype(jnp.float32) * value_branch.astype(jnp.float32)).astype(jnp.bfloat16)
    rim = shifted(kv, "tok", 1)
    partial = lax.dot_general(
        out_weight, cotangent, (((1,), (1,)), ((), ())), preferred_element_type=jnp.float32
    ).astype(jnp.bfloat16)
    filters_rev = jnp.roll(filters[:, ::-1], 1, axis=1)
    conv, gated = pl.pallas_call(
        functools.partial(forward_kernel, group_size),
        grid=(width // tile,),
        in_specs=[channels, channels, channels, by_group],
        out_specs=[channels, channels],
        out_shape=[jax.ShapeDtypeStruct((length, width), jnp.float32), wide],
        cost_estimate=pl.CostEstimate(flops=flops, bytes_accessed=10 * length * width, transcendentals=0),
    )(queries, kv, rim, filters_rev)
    grad_gated = (
        lax.psum_scatter(partial, "wid", scatter_dimension=0, tiled=True).astype(jnp.float32).T
    )
    layer_out = jnp.dot(
        lax.all_gather(gated, "wid", axis=1, tiled=True),
        out_weight,
        preferred_element_type=jnp.float32,
    ).astype(jnp.bfloat16)
    grad_conv = (grad_gated * queries.astype(jnp.float32)).astype(jnp.bfloat16)
    grad_queries = (grad_gated * conv).astype(jnp.bfloat16)
    grad_next = shifted(grad_conv, "tok", -1)
    grad_keys, grad_values, local_terms = pl.pallas_call(
        functools.partial(backward_kernel, group_size),
        grid=(width // tile,),
        in_specs=[channels] * 5 + [by_group],
        out_specs=[channels, channels, by_group],
        out_shape=[wide, wide, jax.ShapeDtypeStruct((groups, kernel), jnp.float32)],
        cost_estimate=pl.CostEstimate(flops=2 * flops, bytes_accessed=14 * length * width, transcendentals=0),
    )(key_branch, value_branch, rim, grad_conv, grad_next, filters)
    scale_factor = 1.0 / math.sqrt(length * lax.axis_size("tok") * group_size)
    grad_filters = lax.psum(local_terms, "tok") * scale_factor
    return (layer_out, grad_queries, grad_keys, grad_values, grad_filters)


def solution(mesh):
    return jax.shard_map(
        local,
        mesh=mesh,
        in_specs=(
            P("tok", "wid"),
            P("tok", "wid"),
            P("tok", "wid"),
            P("wid", None),
            P(None, "wid"),
            P("tok", "wid"),
        ),
        out_specs=(
            P("tok", "wid"),
            P("tok", "wid"),
            P("tok", "wid"),
            P("tok", "wid"),
            P("wid", None),
        ),
        check_vma=False,
    )
```

```python
import functools
import math

import jax
import jax.numpy as jnp
from jax import lax
from jax.experimental import pallas as pl
from jax.experimental.pallas import tpu as pltpu
from jax.sharding import PartitionSpec as P


def iota(shape, dim):
    return lax.broadcasted_iota(jnp.int32, shape, dim)


def circulant(row, kernel):
    return pltpu.roll(jnp.broadcast_to(row, (kernel, kernel)), 0, 1, stride=1, stride_axis=0)


def forward_tile(filters_rev, extended, group_size):
    groups, kernel = filters_rev.shape
    tile = extended.shape[1]
    row, lane = iota((kernel, kernel), 0), iota((kernel, kernel), 1)
    now = lane <= row
    owner = iota((kernel, tile), 1) // group_size
    result = jnp.zeros((kernel, tile), jnp.float32)
    for g in range(groups):
        ring = circulant(filters_rev[g : g + 1], kernel)
        both = jnp.concatenate(
            [jnp.where(now, 0.0, ring).astype(jnp.bfloat16), jnp.where(now, ring, 0.0).astype(jnp.bfloat16)],
            axis=1,
        )
        part = jnp.dot(both, extended, preferred_element_type=jnp.float32)
        result = jnp.where(owner == g, part, result)
    return result


def backward_tile(filters, grads, group_size):
    groups, kernel = filters.shape
    tile = grads.shape[1]
    row, lane = iota((kernel, kernel), 0), iota((kernel, kernel), 1)
    now = row <= lane
    owner = iota((kernel, tile), 1) // group_size
    result = jnp.zeros((kernel, tile), jnp.float32)
    for g in range(groups):
        ring = circulant(filters[g : g + 1], kernel)
        both = jnp.concatenate(
            [jnp.where(now, ring, 0.0).astype(jnp.bfloat16), jnp.where(now, 0.0, ring).astype(jnp.bfloat16)],
            axis=1,
        )
        part = jnp.dot(both, grads, preferred_element_type=jnp.float32)
        result = jnp.where(owner == g, part, result)
    return result


def filter_tile(extended, own_grads, groups, group_size):
    kernel, tile = own_grads.shape
    row, lane = iota((kernel, kernel), 0), iota((kernel, kernel), 1)
    now = row + lane >= kernel - 1
    owner = iota((2 * kernel, tile), 1) // group_size
    mirror = jnp.where(row + lane == kernel - 1, 1.0, 0.0).astype(jnp.bfloat16)
    extended = jnp.concatenate(
        [
            jnp.dot(mirror, half, preferred_element_type=jnp.float32).astype(jnp.bfloat16)
            for half in (extended[:kernel], extended[kernel:])
        ],
        axis=0,
    )
    rows = []
    for g in range(groups):
        part = lax.dot_general(
            jnp.where(owner == g, extended, jnp.zeros_like(extended)),
            own_grads,
            (((1,), (1,)), ((), ())),
            preferred_element_type=jnp.float32,
        )
        square = jnp.where(now, part[kernel:], part[:kernel])
        aligned = pltpu.roll(square, 1, 1, stride=1, stride_axis=0)
        rows.append(jnp.sum(aligned, axis=0, keepdims=True))
    return jnp.concatenate(rows, axis=0)


def kernel(
    sizes,
    q_ref, k_ref, v_ref, f_ref, w_ref, cot_ref,
    out_ref, gq_ref, gk_ref, gv_ref, gf_ref,
    w_buf, kv_buf, rim_buf, conv_buf, part_buf, sib_out, sib_in, pre_out, pre_in,
    gather, total, gc_buf, gcn_buf, frev_buf, local_buf, terms_buf, all_buf,
    w_sem, kv_send, kv_recv, sib_send, sib_recv, pre_send, pre_recv,
    own_send, own_recv, peer_send, peer_recv, fwd_send, fwd_recv, gc_send, gc_recv,
    term_send, term_recv, sum_send, sum_recv,
):
    n_tok, n_wid, tile, chunk, halves, owners = sizes
    length, width = q_ref.shape
    groups, kernel_size = f_ref.shape
    group_size = width // groups
    tile_groups = tile // group_size
    per_block = width // chunk
    chips = n_wid // 2
    rows = groups // owners
    half = width // halves
    tok, me = lax.axis_index("tok"), lax.axis_index("wid")
    chip, core = me // 2, lax.rem(me, 2)
    sibling = chip * 2 + 1 - core
    other_chips = [lax.rem(chip + off, chips) for off in range(1, chips)]
    other_toks = [lax.rem(tok + off, n_tok) for off in range(1, n_tok)]
    order = []
    for p in other_chips + [chip]:
        order += [p * 2 + 1 - core, p * 2 + core]

    def w_copy(position, j):
        at = pl.ds(pl.multiple_of(order[position] * width + j * chunk, chunk), chunk)
        return pltpu.make_async_copy(w_ref.at[at], w_buf.at[at], w_sem.at[position * per_block + j])

    for position in range(n_wid):
        for j in range(per_block):
            w_copy(position, j).start()

    def remote(src, dst, send, recv, **where):
        return pltpu.make_async_remote_copy(
            src_ref=src, dst_ref=dst, send_sem=send, recv_sem=recv,
            device_id=where, device_id_type=pl.DeviceIdType.MESH,
        )

    barrier = pltpu.get_barrier_semaphore()
    for where in (
        [{"wid": sibling}] + [{"wid": p * 2 + core} for p in other_chips] + [{"tok": t} for t in other_toks]
    ):
        pl.semaphore_signal(barrier, inc=1, device_id=where, device_id_type=pl.DeviceIdType.MESH)
    pl.semaphore_wait(barrier, 1 + len(other_chips) + len(other_toks))

    kv_buf[...] = (k_ref[...].astype(jnp.float32) * v_ref[...].astype(jnp.float32)).astype(jnp.bfloat16)
    kv_copy = remote(kv_buf, rim_buf, kv_send, kv_recv, tok=lax.rem(tok + 1, n_tok))
    has_next, has_previous = tok < n_tok - 1, tok > 0

    @pl.when(has_next)
    def _():
        kv_copy.start()

    cot = cot_ref[...]

    def sib_copy(p):
        return remote(sib_out.at[p], sib_in.at[p], sib_send.at[p], sib_recv.at[p], wid=sibling)

    def pre_copy(p, slot):
        return remote(pre_out.at[p], pre_in.at[slot], pre_send.at[p], pre_recv.at[slot], wid=p * 2 + core)

    for position in range(n_wid):
        block = order[position]

        @pl.loop(0, per_block)
        def _(j):
            w_copy(position, j).wait()
            at = pl.ds(pl.multiple_of(block * width + j * chunk, chunk), chunk)
            part_buf[:, pl.ds(pl.multiple_of(j * chunk, chunk), chunk)] = lax.dot_general(
                cot, w_buf[at, :], (((1,), (1,)), ((), ())), preferred_element_type=jnp.float32
            )

        p = (other_chips + [chip])[position // 2]
        if position % 2 == 0:
            sib_out[p] = part_buf[...].astype(jnp.bfloat16)
            sib_copy(p).start()
        elif position < n_wid - 1:
            sib_copy(p).wait_recv()
            pre_out[p] = (part_buf[...] + sib_in[p].astype(jnp.float32)).astype(jnp.bfloat16)
            pre_copy(p, chip).start()

    flip = jnp.where(
        lax.rem(iota((kernel_size, kernel_size), 0) + iota((kernel_size, kernel_size), 1), kernel_size) == 0, 1.0, 0.0
    ).astype(jnp.bfloat16)
    frev_buf[...] = jnp.dot(f_ref[...].astype(jnp.bfloat16), flip, preferred_element_type=jnp.float32)

    @pl.when(has_previous)
    def _():
        kv_copy.wait_recv()

    @pl.when(jnp.logical_not(has_previous))
    def _():
        rim_buf[...] = jnp.zeros_like(rim_buf)

    def own_copy(h, slot):
        at = pl.ds(h * half, half)
        return remote(gather.at[me, :, at], gather.at[slot, :, at], own_send.at[h], own_recv.at[h], wid=sibling)

    def peer_copy(p, h, slot, slot_chip):
        at = pl.ds(h * half, half)
        return remote(
            gather.at[me, :, at], gather.at[slot, :, at],
            peer_send.at[p * halves + h], peer_recv.at[slot_chip * halves + h], wid=p * 2 + core,
        )

    def fwd_copy(p, h, slot):
        at = pl.ds(h * half, half)
        return remote(
            gather.at[p * 2 + core, :, at], gather.at[slot, :, at],
            fwd_send.at[p * halves + h], fwd_recv.at[p * halves + h], wid=sibling,
        )

    for h in range(halves):

        @pl.loop(h * (half // tile), (h + 1) * (half // tile))
        def _(i):
            at = pl.ds(pl.multiple_of(i * tile, tile), tile)
            which = pl.ds(pl.multiple_of(i * tile_groups, tile_groups), tile_groups)
            extended = jnp.concatenate([rim_buf[:, at], kv_buf[:, at]], axis=0)
            conv = forward_tile(frev_buf[which, :], extended, group_size)
            conv_buf[:, at] = conv
            gather[me, :, at] = (q_ref[:, at].astype(jnp.float32) * conv).astype(jnp.bfloat16)

        for p in other_chips:
            peer_copy(p, h, me, chip).start()
        own_copy(h, me).start()

    sib_copy(chip).wait_recv()
    for p in other_chips:
        pre_copy(p, p).wait_recv()

    @pl.loop(0, width // tile)
    def _(i):
        at = pl.ds(pl.multiple_of(i * tile, tile), tile)
        grad_gated = part_buf[:, at] + sib_in[chip, :, at].astype(jnp.float32)
        for p in other_chips:
            grad_gated = grad_gated + pre_in[p, :, at].astype(jnp.float32)
        gc_buf[:, at] = (grad_gated * q_ref[:, at].astype(jnp.float32)).astype(jnp.bfloat16)
        gq_ref[:, at] = (grad_gated * conv_buf[:, at]).astype(jnp.bfloat16)

    gc_copy = remote(gc_buf, gcn_buf, gc_send, gc_recv, tok=lax.rem(tok + n_tok - 1, n_tok))

    @pl.when(has_previous)
    def _():
        gc_copy.start()

    @pl.loop(0, width // tile)
    def _(i):
        at = pl.ds(pl.multiple_of(i * tile, tile), tile)
        which = pl.ds(pl.multiple_of(i * tile_groups, tile_groups), tile_groups)
        extended = jnp.concatenate([rim_buf[:, at], kv_buf[:, at]], axis=0)
        local_buf[which, :] = filter_tile(extended, gc_buf[:, at], tile_groups, group_size)

    def owned(t):
        return pl.ds(pl.multiple_of(t * rows, rows), rows)

    def term_copy(t, slot):
        return remote(local_buf.at[owned(lax.rem(t, owners))], terms_buf.at[slot], term_send.at[t], term_recv.at[slot], tok=t)

    def sum_copy(t, owner):
        return remote(all_buf.at[owned(owner)], all_buf.at[owned(owner)], sum_send.at[t], sum_recv.at[owner], tok=t)

    def if_owner(t, action):
        if owners == n_tok:
            action()
        else:
            pl.when(t < owners)(action)

    for t in other_toks:
        if_owner(t, lambda t=t: term_copy(t, tok).start())

    def project(block, start, depth, first):
        @pl.loop(0, width // chunk)
        def _(j):
            at = pl.ds(pl.multiple_of(j * chunk, chunk), chunk)
            deep = pl.ds(pl.multiple_of(block * width + start, depth), depth)
            product = jnp.dot(
                gather[block, :, pl.ds(start, depth)], w_buf[deep, at], preferred_element_type=jnp.float32
            )
            total[:, at] = product if first else total[:, at] + product

    project(me, 0, width, True)
    for h in range(halves):
        own_copy(h, sibling).wait_recv()

    def sum_terms():
        for t in other_toks:
            term_copy(t, t).wait_recv()
        terms_buf[tok] = local_buf[owned(tok), :]
        all_buf[owned(tok), :] = jnp.sum(terms_buf[...], axis=0)
        for t in other_toks:
            sum_copy(t, tok).start()

    for h in range(halves):
        for p in other_chips:
            peer_copy(p, h, p * 2 + core, p).wait_recv()
            fwd_copy(p, h, p * 2 + core).start()
    project(sibling, 0, width, False)
    for p in other_chips:
        project(p * 2 + core, 0, width, False)
    if_owner(tok, sum_terms)
    for p in other_chips:
        for h in range(halves):
            fwd_copy(p, h, p * 2 + 1 - core).wait_recv()
        project(p * 2 + 1 - core, 0, width, False)
    out_ref[...] = total[...].astype(jnp.bfloat16)

    @pl.when(has_next)
    def _():
        gc_copy.wait_recv()

    @pl.when(jnp.logical_not(has_next))
    def _():
        gcn_buf[...] = jnp.zeros_like(gcn_buf)

    @pl.loop(0, width // tile)
    def _(i):
        at = pl.ds(pl.multiple_of(i * tile, tile), tile)
        which = pl.ds(pl.multiple_of(i * tile_groups, tile_groups), tile_groups)
        grads = jnp.concatenate([gc_buf[:, at], gcn_buf[:, at]], axis=0)
        grad_kv = backward_tile(f_ref[which, :], grads, group_size)
        gk_ref[:, at] = (grad_kv * v_ref[:, at].astype(jnp.float32)).astype(jnp.bfloat16)
        gv_ref[:, at] = (grad_kv * k_ref[:, at].astype(jnp.float32)).astype(jnp.bfloat16)

    for t in other_toks:
        if_owner(t, lambda t=t: sum_copy(t, t).wait_recv())
    gf_ref[...] = all_buf[...] * (1.0 / math.sqrt(length * n_tok * group_size))

    pl.when(has_next)(lambda: kv_copy.wait_send())
    pl.when(has_previous)(lambda: gc_copy.wait_send())
    for p in other_chips + [chip]:
        sib_copy(p).wait_send()
    for p in other_chips:
        pre_copy(p, chip).wait_send()
    for h in range(halves):
        own_copy(h, me).wait_send()
        for p in other_chips:
            peer_copy(p, h, me, chip).wait_send()
            fwd_copy(p, h, p * 2 + core).wait_send()
    for t in other_toks:
        if_owner(t, lambda t=t: term_copy(t, tok).wait_send())

    def sums_sent():
        for t in other_toks:
            sum_copy(t, tok).wait_send()

    if_owner(tok, sums_sent)


def local(queries, key_branch, value_branch, filters, out_weight, cotangent):
    length, width = queries.shape
    groups, kernel_size = filters.shape
    n_tok, n_wid = lax.axis_size("tok"), lax.axis_size("wid")
    chips = n_wid // 2
    tile, chunk = min(256, width), min(512, width)
    halves = 2 if width // tile % 2 == 0 else 1
    owners = min(n_tok, groups // 8)
    bf16, f32 = jnp.bfloat16, jnp.float32
    wide = jax.ShapeDtypeStruct((length, width), bf16)
    dma = pltpu.SemaphoreType.DMA
    vmem = pl.BlockSpec(memory_space=pltpu.VMEM)
    return pl.pallas_call(
        functools.partial(kernel, (n_tok, n_wid, tile, chunk, halves, owners)),
        in_specs=[vmem] * 4 + [pl.BlockSpec(memory_space=pl.ANY), vmem],
        out_specs=[vmem] * 5,
        out_shape=[wide] * 4 + [jax.ShapeDtypeStruct(filters.shape, f32)],
        scratch_shapes=[
            pltpu.VMEM(out_weight.shape, bf16),
            pltpu.VMEM((length, width), bf16),
            pltpu.VMEM((length, width), bf16),
            pltpu.VMEM((length, width), f32),
            pltpu.VMEM((length, width), f32),
            pltpu.VMEM((chips, length, width), bf16),
            pltpu.VMEM((chips, length, width), bf16),
            pltpu.VMEM((chips, length, width), bf16),
            pltpu.VMEM((chips, length, width), bf16),
            pltpu.VMEM((n_wid, length, width), bf16),
            pltpu.VMEM((length, width), f32),
            pltpu.VMEM((length, width), bf16),
            pltpu.VMEM((length, width), bf16),
            pltpu.VMEM(filters.shape, f32),
            pltpu.VMEM(filters.shape, f32),
            pltpu.VMEM((n_tok, groups // owners, kernel_size), f32),
            pltpu.VMEM(filters.shape, f32),
            dma((n_wid * (width // chunk),)),
            dma, dma,
            dma((chips,)), dma((chips,)), dma((chips,)), dma((chips,)),
            dma((halves,)), dma((halves,)),
            dma((chips * halves,)), dma((chips * halves,)), dma((chips * halves,)), dma((chips * halves,)),
            dma, dma,
            dma((n_tok,)), dma((n_tok,)), dma((n_tok,)), dma((n_tok,)),
        ],
        compiler_params=pltpu.CompilerParams(
            collective_id=0, has_side_effects=True, vmem_limit_bytes=60 * 2**20
        ),
        cost_estimate=pl.CostEstimate(
            flops=4 * length * width * width * n_wid, bytes_accessed=2 * width * width * n_wid, transcendentals=0
        ),
    )(queries, key_branch, value_branch, filters, out_weight, cotangent)


def solution(mesh):
    return jax.shard_map(
        local,
        mesh=mesh,
        in_specs=(
            P("tok", "wid"),
            P("tok", "wid"),
            P("tok", "wid"),
            P("wid", None),
            P(None, "wid"),
            P("tok", "wid"),
        ),
        out_specs=(
            P("tok", "wid"),
            P("tok", "wid"),
            P("tok", "wid"),
            P("tok", "wid"),
            P("wid", None),
        ),
        check_vma=False,
    )
```

```python
import functools
import math

import jax
import jax.numpy as jnp
from jax import lax
from jax.experimental import pallas as pl
from jax.experimental.pallas import tpu as pltpu
from jax.sharding import PartitionSpec as P


def iota(shape, dim):
    return lax.broadcasted_iota(jnp.int32, shape, dim)


def circulant(row, kernel):
    return pltpu.roll(jnp.broadcast_to(row, (kernel, kernel)), 0, 1, stride=1, stride_axis=0)


def as_mask(condition):
    return jnp.where(condition, 1.0, 0.0).astype(jnp.bfloat16)


def conv_tile(filters, data, now, group_size, now_first):
    groups, kernel = filters.shape
    tile = data.shape[1]
    inside, outside = as_mask(now), as_mask(jnp.logical_not(now))
    owner = iota((kernel, tile), 1) // group_size
    result = jnp.zeros((kernel, tile), jnp.float32)
    for g in range(groups):
        ring = circulant(filters[g : g + 1], kernel).astype(jnp.bfloat16)
        pair = [ring * inside, ring * outside] if now_first else [ring * outside, ring * inside]
        part = jnp.dot(jnp.concatenate(pair, axis=1), data, preferred_element_type=jnp.float32)
        result = jnp.where(owner == g, part, result)
    return result


def forward_tile(filters_rev, extended, group_size):
    kernel = filters_rev.shape[1]
    now = iota((kernel, kernel), 1) <= iota((kernel, kernel), 0)
    return conv_tile(filters_rev, extended, now, group_size, False)


def backward_tile(filters, grads, group_size):
    kernel = filters.shape[1]
    now = iota((kernel, kernel), 0) <= iota((kernel, kernel), 1)
    return conv_tile(filters, grads, now, group_size, True)


def filter_tile(extended, own_grads, groups, group_size):
    kernel, tile = own_grads.shape
    row, lane = iota((kernel, kernel), 0), iota((kernel, kernel), 1)
    now = row + lane <= kernel - 1
    owner = iota((kernel, tile), 1) // group_size
    mirrored = jnp.dot(
        as_mask(row + lane == kernel - 1), own_grads, preferred_element_type=jnp.float32
    ).astype(jnp.bfloat16)
    rows = []
    for g in range(groups):
        part = lax.dot_general(
            mirrored * as_mask(owner == g),
            extended,
            (((1,), (1,)), ((), ())),
            preferred_element_type=jnp.float32,
        )
        square = jnp.where(now, part[:, kernel:], part[:, :kernel])
        aligned = pltpu.roll(square, 1, 1, stride=1, stride_axis=0)
        rows.append(jnp.sum(aligned, axis=0, keepdims=True))
    return jnp.concatenate(rows, axis=0)


def kernel(
    sizes,
    q_ref, k_ref, v_ref, f_ref, w_ref, cot_ref,
    out_ref, gq_ref, own_out, next_out, gf_ref,
    w_buf, kv_buf, rim_buf, conv_buf, part_buf, sib_out, sib_in, pre_out, pre_in,
    gather, total, gc_buf, gcn_buf, frev_buf, local_buf, terms_buf, all_buf,
    w_sem, kv_send, kv_recv, sib_send, sib_recv, pre_send, pre_recv,
    own_send, own_recv, peer_send, peer_recv, fwd_send, fwd_recv, gc_send, gc_recv,
    term_send, term_recv, sum_send, sum_recv,
):
    n_tok, n_wid, tile, chunk, halves, owners = sizes
    length, width = q_ref.shape
    groups, kernel_size = f_ref.shape
    group_size = width // groups
    tile_groups = tile // group_size
    half = width // halves
    per_piece = half // chunk
    chips = n_wid // 2
    rows = groups // owners
    tok, me = lax.axis_index("tok"), lax.axis_index("wid")
    chip, core = me // 2, lax.rem(me, 2)
    sibling = chip * 2 + 1 - core
    other_chips = [lax.rem(chip + off, chips) for off in range(1, chips)]
    other_toks = [lax.rem(tok + off, n_tok) for off in range(1, n_tok)]
    order = []
    for p in other_chips + [chip]:
        for h in range(halves):
            order += [(p, p * 2 + 1 - core, h), (p, p * 2 + core, h)]

    def w_copy(position, j):
        start = order[position][1] * width + order[position][2] * half + j * chunk
        at = pl.ds(pl.multiple_of(start, chunk), chunk)
        return pltpu.make_async_copy(w_ref.at[at], w_buf.at[at], w_sem.at[position * per_piece + j])

    for position in range(len(order)):
        for j in range(per_piece):
            w_copy(position, j).start()

    def remote(src, dst, send, recv, **where):
        return pltpu.make_async_remote_copy(
            src_ref=src, dst_ref=dst, send_sem=send, recv_sem=recv,
            device_id=where, device_id_type=pl.DeviceIdType.MESH,
        )

    barrier = pltpu.get_barrier_semaphore()
    for where in (
        [{"wid": sibling}] + [{"wid": p * 2 + core} for p in other_chips] + [{"tok": t} for t in other_toks]
    ):
        pl.semaphore_signal(barrier, inc=1, device_id=where, device_id_type=pl.DeviceIdType.MESH)
    pl.semaphore_wait(barrier, 1 + len(other_chips) + len(other_toks))

    kv_buf[...] = (k_ref[...].astype(jnp.float32) * v_ref[...].astype(jnp.float32)).astype(jnp.bfloat16)
    kv_copy = remote(kv_buf, rim_buf, kv_send, kv_recv, tok=lax.rem(tok + 1, n_tok))
    has_next, has_previous = tok < n_tok - 1, tok > 0

    @pl.when(has_next)
    def _():
        kv_copy.start()

    cot = cot_ref[...]

    def sib_copy(p, h):
        at, sem = pl.ds(h * half, half), p * halves + h
        return remote(sib_out.at[p, :, at], sib_in.at[p, :, at], sib_send.at[sem], sib_recv.at[sem], wid=sibling)

    def pre_copy(p, slot, h):
        at = pl.ds(h * half, half)
        return remote(
            pre_out.at[p, :, at], pre_in.at[slot, :, at],
            pre_send.at[p * halves + h], pre_recv.at[slot * halves + h], wid=p * 2 + core,
        )

    def send_sum(p, h):
        at = pl.ds(h * half, half)
        sib_copy(p, h).wait_recv()
        pre_out[p, :, at] = (part_buf[:, at] + sib_in[p, :, at].astype(jnp.float32)).astype(jnp.bfloat16)
        pre_copy(p, chip, h).start()

    waiting = None
    for position, (p, block, h) in enumerate(order):

        @pl.loop(0, per_piece)
        def _(j):
            w_copy(position, j).wait()
            at = pl.ds(pl.multiple_of(block * width + h * half + j * chunk, chunk), chunk)
            part_buf[:, pl.ds(pl.multiple_of(h * half + j * chunk, chunk), chunk)] = lax.dot_general(
                cot, w_buf[at, :], (((1,), (1,)), ((), ())), preferred_element_type=jnp.float32
            )

        if position % 2 == 0:
            at = pl.ds(h * half, half)
            sib_out[p, :, at] = part_buf[:, at].astype(jnp.bfloat16)
            sib_copy(p, h).start()
            if waiting is not None:
                send_sum(*waiting)
                waiting = None
        elif position < 2 * halves * (chips - 1):
            waiting = (p, h)

    flip = jnp.where(
        lax.rem(iota((kernel_size, kernel_size), 0) + iota((kernel_size, kernel_size), 1), kernel_size) == 0, 1.0, 0.0
    ).astype(jnp.bfloat16)
    frev_buf[...] = jnp.dot(f_ref[...].astype(jnp.bfloat16), flip, preferred_element_type=jnp.float32)

    @pl.when(has_previous)
    def _():
        kv_copy.wait_recv()

    @pl.when(jnp.logical_not(has_previous))
    def _():
        rim_buf[...] = jnp.zeros_like(rim_buf)

    def own_copy(h, slot):
        at = pl.ds(h * half, half)
        return remote(gather.at[me, :, at], gather.at[slot, :, at], own_send.at[h], own_recv.at[h], wid=sibling)

    def peer_copy(p, h, slot, slot_chip):
        at = pl.ds(h * half, half)
        return remote(
            gather.at[me, :, at], gather.at[slot, :, at],
            peer_send.at[p * halves + h], peer_recv.at[slot_chip * halves + h], wid=p * 2 + core,
        )

    def fwd_copy(p, h, slot):
        at = pl.ds(h * half, half)
        return remote(
            gather.at[p * 2 + core, :, at], gather.at[slot, :, at],
            fwd_send.at[p * halves + h], fwd_recv.at[p * halves + h], wid=sibling,
        )

    for h in range(halves):

        @pl.loop(h * (half // tile), (h + 1) * (half // tile))
        def _(i):
            at = pl.ds(pl.multiple_of(i * tile, tile), tile)
            which = pl.ds(pl.multiple_of(i * tile_groups, tile_groups), tile_groups)
            extended = jnp.concatenate([rim_buf[:, at], kv_buf[:, at]], axis=0)
            conv = forward_tile(frev_buf[which, :], extended, group_size)
            conv_buf[:, at] = conv
            gather[me, :, at] = (q_ref[:, at].astype(jnp.float32) * conv).astype(jnp.bfloat16)

        for p in other_chips:
            peer_copy(p, h, me, chip).start()
        own_copy(h, me).start()

    for h in range(halves):
        sib_copy(chip, h).wait_recv()
        for p in other_chips:
            pre_copy(p, p, h).wait_recv()

    @pl.loop(0, width // tile)
    def _(i):
        at = pl.ds(pl.multiple_of(i * tile, tile), tile)
        grad_gated = part_buf[:, at] + sib_in[chip, :, at].astype(jnp.float32)
        for p in other_chips:
            grad_gated = grad_gated + pre_in[p, :, at].astype(jnp.float32)
        gc_buf[:, at] = (grad_gated * q_ref[:, at].astype(jnp.float32)).astype(jnp.bfloat16)
        gq_ref[:, at] = (grad_gated * conv_buf[:, at]).astype(jnp.bfloat16)

    gc_copy = remote(gc_buf, gcn_buf, gc_send, gc_recv, tok=lax.rem(tok + n_tok - 1, n_tok))

    @pl.when(has_previous)
    def _():
        gc_copy.start()

    @pl.loop(0, width // tile)
    def _(i):
        at = pl.ds(pl.multiple_of(i * tile, tile), tile)
        which = pl.ds(pl.multiple_of(i * tile_groups, tile_groups), tile_groups)
        extended = jnp.concatenate([rim_buf[:, at], kv_buf[:, at]], axis=0)
        local_buf[which, :] = filter_tile(extended, gc_buf[:, at], tile_groups, group_size)

    local_buf[...] = jnp.dot(
        local_buf[...], flip.astype(jnp.float32), preferred_element_type=jnp.float32, precision=lax.Precision.HIGHEST
    )

    def owned(t):
        return pl.ds(pl.multiple_of(t * rows, rows), rows)

    def term_copy(t, slot):
        return remote(local_buf.at[owned(lax.rem(t, owners))], terms_buf.at[slot], term_send.at[t], term_recv.at[slot], tok=t)

    def sum_copy(t, owner):
        return remote(all_buf.at[owned(owner)], all_buf.at[owned(owner)], sum_send.at[t], sum_recv.at[owner], tok=t)

    def if_owner(t, action):
        if owners == n_tok:
            action()
        else:
            pl.when(t < owners)(action)

    for t in other_toks:
        if_owner(t, lambda t=t: term_copy(t, tok).start())

    def project(block, start, depth, first):
        @pl.loop(0, width // chunk)
        def _(j):
            at = pl.ds(pl.multiple_of(j * chunk, chunk), chunk)
            deep = pl.ds(pl.multiple_of(block * width + start, depth), depth)
            product = jnp.dot(
                gather[block, :, pl.ds(start, depth)], w_buf[deep, at], preferred_element_type=jnp.float32
            )
            total[:, at] = product if first else total[:, at] + product

    project(me, 0, width, True)
    for h in range(halves):
        own_copy(h, sibling).wait_recv()

    def sum_terms():
        for t in other_toks:
            term_copy(t, t).wait_recv()
        terms_buf[tok] = local_buf[owned(tok), :]
        all_buf[owned(tok), :] = jnp.sum(terms_buf[...], axis=0)
        for t in other_toks:
            sum_copy(t, tok).start()

    for h in range(halves):
        for p in other_chips:
            peer_copy(p, h, p * 2 + core, p).wait_recv()
            fwd_copy(p, h, p * 2 + core).start()
    project(sibling, 0, width, False)
    for p in other_chips:
        project(p * 2 + core, 0, width, False)
    if_owner(tok, sum_terms)
    for p in other_chips:
        for h in range(halves):
            fwd_copy(p, h, p * 2 + 1 - core).wait_recv()
        project(p * 2 + 1 - core, 0, width, False)
    out_ref[...] = total[...].astype(jnp.bfloat16)

    @pl.when(has_next)
    def _():
        gc_copy.wait_recv()

    @pl.when(jnp.logical_not(has_next))
    def _():
        gcn_buf[...] = jnp.zeros_like(gcn_buf)

    own_out[...] = gc_buf[...]
    next_out[...] = gcn_buf[...]
    for t in other_toks:
        if_owner(t, lambda t=t: sum_copy(t, t).wait_recv())
    gf_ref[...] = all_buf[...]

    pl.when(has_next)(lambda: kv_copy.wait_send())
    pl.when(has_previous)(lambda: gc_copy.wait_send())
    for h in range(halves):
        for p in other_chips + [chip]:
            sib_copy(p, h).wait_send()
        for p in other_chips:
            pre_copy(p, chip, h).wait_send()
    for h in range(halves):
        own_copy(h, me).wait_send()
        for p in other_chips:
            peer_copy(p, h, me, chip).wait_send()
            fwd_copy(p, h, p * 2 + core).wait_send()
    for t in other_toks:
        if_owner(t, lambda t=t: term_copy(t, tok).wait_send())

    def sums_sent():
        for t in other_toks:
            sum_copy(t, tok).wait_send()

    if_owner(tok, sums_sent)


def last_kernel(
    group_size, tile, scale, out_ref, gq_ref, own_ref, next_ref, sums_ref, k_ref, v_ref, f_ref,
    out, gq, gk, gv, gf,
):
    out[...] = out_ref[...]
    gq[...] = gq_ref[...]
    gf[...] = sums_ref[...] * scale
    tile_groups = tile // group_size

    @pl.loop(0, k_ref.shape[1] // tile)
    def _(i):
        at = pl.ds(pl.multiple_of(i * tile, tile), tile)
        which = pl.ds(pl.multiple_of(i * tile_groups, tile_groups), tile_groups)
        grads = jnp.concatenate([own_ref[:, at], next_ref[:, at]], axis=0)
        grad_kv = backward_tile(f_ref[which, :], grads, group_size)
        gk[:, at] = (grad_kv * v_ref[:, at].astype(jnp.float32)).astype(jnp.bfloat16)
        gv[:, at] = (grad_kv * k_ref[:, at].astype(jnp.float32)).astype(jnp.bfloat16)


def local(queries, key_branch, value_branch, filters, out_weight, cotangent):
    length, width = queries.shape
    groups, kernel_size = filters.shape
    n_tok, n_wid = lax.axis_size("tok"), lax.axis_size("wid")
    chips = n_wid // 2
    group_size = width // groups
    tile, halves = min(128, width // 2), 2
    chunk = min(512, width // halves)
    step = min(512, width)
    owners = min(n_tok, groups // 8)
    bf16, f32 = jnp.bfloat16, jnp.float32
    wide = jax.ShapeDtypeStruct((length, width), bf16)
    dma = pltpu.SemaphoreType.DMA
    vmem = pl.BlockSpec(memory_space=pltpu.VMEM)
    results = pl.pallas_call(
        functools.partial(kernel, (n_tok, n_wid, tile, chunk, halves, owners)),
        in_specs=[vmem] * 4 + [pl.BlockSpec(memory_space=pl.ANY), vmem],
        out_specs=[vmem] * 5,
        out_shape=[wide] * 4 + [jax.ShapeDtypeStruct(filters.shape, f32)],
        scratch_shapes=[
            pltpu.VMEM(out_weight.shape, bf16),
            pltpu.VMEM((length, width), bf16),
            pltpu.VMEM((length, width), bf16),
            pltpu.VMEM((length, width), f32),
            pltpu.VMEM((length, width), f32),
            pltpu.VMEM((chips, length, width), bf16),
            pltpu.VMEM((chips, length, width), bf16),
            pltpu.VMEM((chips, length, width), bf16),
            pltpu.VMEM((chips, length, width), bf16),
            pltpu.VMEM((n_wid, length, width), bf16),
            pltpu.VMEM((length, width), f32),
            pltpu.VMEM((length, width), bf16),
            pltpu.VMEM((length, width), bf16),
            pltpu.VMEM(filters.shape, f32),
            pltpu.VMEM(filters.shape, f32),
            pltpu.VMEM((n_tok, groups // owners, kernel_size), f32),
            pltpu.VMEM(filters.shape, f32),
            dma((n_wid * (width // chunk),)),
            dma, dma,
            dma((chips * halves,)), dma((chips * halves,)), dma((chips * halves,)), dma((chips * halves,)),
            dma((halves,)), dma((halves,)),
            dma((chips * halves,)), dma((chips * halves,)), dma((chips * halves,)), dma((chips * halves,)),
            dma, dma,
            dma((n_tok,)), dma((n_tok,)), dma((n_tok,)), dma((n_tok,)),
        ],
        compiler_params=pltpu.CompilerParams(
            collective_id=0, has_side_effects=True, vmem_limit_bytes=60 * 2**20
        ),
        cost_estimate=pl.CostEstimate(
            flops=4 * length * width * width * n_wid, bytes_accessed=2 * width * width * n_wid, transcendentals=0
        ),
    )(queries, key_branch, value_branch, filters, out_weight, cotangent)
    channels = pl.BlockSpec((length, step), lambda i: (0, i))
    by_group = pl.BlockSpec((step // group_size, kernel_size), lambda i: (i, 0))
    scale = 1.0 / math.sqrt(length * n_tok * group_size)
    return pl.pallas_call(
        functools.partial(last_kernel, group_size, tile, scale),
        grid=(width // step,),
        in_specs=[channels] * 4 + [by_group, channels, channels, by_group],
        out_specs=[channels] * 4 + [by_group],
        out_shape=[wide] * 4 + [jax.ShapeDtypeStruct(filters.shape, f32)],
    )(*results, key_branch, value_branch, filters)


def solution(mesh):
    return jax.shard_map(
        local,
        mesh=mesh,
        in_specs=(
            P("tok", "wid"),
            P("tok", "wid"),
            P("tok", "wid"),
            P("wid", None),
            P(None, "wid"),
            P("tok", "wid"),
        ),
        out_specs=(
            P("tok", "wid"),
            P("tok", "wid"),
            P("tok", "wid"),
            P("tok", "wid"),
            P("wid", None),
        ),
        check_vma=False,
    )
```

```python
import functools
import math

import jax
import jax.numpy as jnp
from jax import lax
from jax.experimental import pallas as pl
from jax.experimental.pallas import tpu as pltpu
from jax.sharding import PartitionSpec as P


def iota(shape, dim):
    return lax.broadcasted_iota(jnp.int32, shape, dim)


def circulant(row, kernel):
    return pltpu.roll(jnp.broadcast_to(row, (kernel, kernel)), 0, 1, stride=1, stride_axis=0)


def as_mask(condition):
    return jnp.where(condition, 1.0, 0.0).astype(jnp.bfloat16)


def conv_tile(filters, data, now, group_size, now_first):
    groups, kernel = filters.shape
    tile = data.shape[1]
    inside, outside = as_mask(now), as_mask(jnp.logical_not(now))
    owner = iota((kernel, tile), 1) // group_size
    result = jnp.zeros((kernel, tile), jnp.float32)
    for g in range(groups):
        ring = circulant(filters[g : g + 1], kernel).astype(jnp.bfloat16)
        pair = [ring * inside, ring * outside] if now_first else [ring * outside, ring * inside]
        part = jnp.dot(jnp.concatenate(pair, axis=1), data, preferred_element_type=jnp.float32)
        result = jnp.where(owner == g, part, result)
    return result


def forward_tile(filters_rev, extended, group_size):
    kernel = filters_rev.shape[1]
    now = iota((kernel, kernel), 1) <= iota((kernel, kernel), 0)
    return conv_tile(filters_rev, extended, now, group_size, False)


def backward_tile(filters, grads, group_size):
    kernel = filters.shape[1]
    now = iota((kernel, kernel), 0) <= iota((kernel, kernel), 1)
    return conv_tile(filters, grads, now, group_size, True)


def filter_tile(extended, own_grads, groups, group_size):
    kernel, tile = own_grads.shape
    row, lane = iota((kernel, kernel), 0), iota((kernel, kernel), 1)
    now = row + lane <= kernel - 1
    owner = iota((kernel, tile), 1) // group_size
    mirrored = jnp.dot(
        as_mask(row + lane == kernel - 1), own_grads, preferred_element_type=jnp.float32
    ).astype(jnp.bfloat16)
    rows = []
    for g in range(groups):
        part = lax.dot_general(
            mirrored * as_mask(owner == g),
            extended,
            (((1,), (1,)), ((), ())),
            preferred_element_type=jnp.float32,
        )
        square = jnp.where(now, part[:, kernel:], part[:, :kernel])
        aligned = pltpu.roll(square, 1, 1, stride=1, stride_axis=0)
        rows.append(jnp.sum(aligned, axis=0, keepdims=True))
    return jnp.concatenate(rows, axis=0)


def kernel(
    sizes,
    q_ref, k_ref, v_ref, f_ref, w_ref, cot_ref,
    out_ref, gq_ref, own_out, next_out, gf_ref,
    w_buf, kv_buf, rim_buf, conv_buf, part_buf, sib_out, sib_in, pre_out, pre_in,
    gather, total, gc_buf, gcn_buf, frev_buf, local_buf, terms_buf, all_buf,
    w_sem, kv_send, kv_recv, sib_send, sib_recv, pre_send, pre_recv,
    own_send, own_recv, peer_send, peer_recv, fwd_send, fwd_recv, gc_send, gc_recv,
    term_send, term_recv, sum_send, sum_recv,
):
    n_tok, n_wid, tile, chunk, halves, owners = sizes
    length, width = q_ref.shape
    groups, kernel_size = f_ref.shape
    group_size = width // groups
    tile_groups = tile // group_size
    half = width // halves
    per_piece = half // chunk
    chips = n_wid // 2
    rows = groups // owners
    tok, me = lax.axis_index("tok"), lax.axis_index("wid")
    chip, core = me // 2, lax.rem(me, 2)
    sibling = chip * 2 + 1 - core
    other_chips = [lax.rem(chip + off, chips) for off in range(1, chips)]
    other_toks = [lax.rem(tok + off, n_tok) for off in range(1, n_tok)]
    order = []
    for p in other_chips + [chip]:
        for h in range(halves):
            order += [(p, p * 2 + 1 - core, h), (p, p * 2 + core, h)]

    def w_copy(position, j):
        start = order[position][1] * width + order[position][2] * half + j * chunk
        at = pl.ds(pl.multiple_of(start, chunk), chunk)
        return pltpu.make_async_copy(w_ref.at[at], w_buf.at[at], w_sem.at[position * per_piece + j])

    for position in range(len(order)):
        for j in range(per_piece):
            w_copy(position, j).start()

    def remote(src, dst, send, recv, **where):
        return pltpu.make_async_remote_copy(
            src_ref=src, dst_ref=dst, send_sem=send, recv_sem=recv,
            device_id=where, device_id_type=pl.DeviceIdType.MESH,
        )

    barrier = pltpu.get_barrier_semaphore()
    for where in (
        [{"wid": sibling}] + [{"wid": p * 2 + core} for p in other_chips] + [{"tok": t} for t in other_toks]
    ):
        pl.semaphore_signal(barrier, inc=1, device_id=where, device_id_type=pl.DeviceIdType.MESH)
    pl.semaphore_wait(barrier, 1 + len(other_chips) + len(other_toks))

    kv_buf[...] = (k_ref[...].astype(jnp.float32) * v_ref[...].astype(jnp.float32)).astype(jnp.bfloat16)
    kv_copy = remote(kv_buf, rim_buf, kv_send, kv_recv, tok=lax.rem(tok + 1, n_tok))
    has_next, has_previous = tok < n_tok - 1, tok > 0

    @pl.when(has_next)
    def _():
        kv_copy.start()

    cot = cot_ref[...]

    def sib_copy(p, h):
        at, sem = pl.ds(h * half, half), p * halves + h
        return remote(sib_out.at[p, :, at], sib_in.at[p, :, at], sib_send.at[sem], sib_recv.at[sem], wid=sibling)

    def pre_copy(p, slot, h):
        at = pl.ds(h * half, half)
        return remote(
            pre_out.at[p, :, at], pre_in.at[slot, :, at],
            pre_send.at[p * halves + h], pre_recv.at[slot * halves + h], wid=p * 2 + core,
        )

    def send_sum(p, h):
        at = pl.ds(h * half, half)
        sib_copy(p, h).wait_recv()
        pre_out[p, :, at] = (part_buf[:, at] + sib_in[p, :, at].astype(jnp.float32)).astype(jnp.bfloat16)
        pre_copy(p, chip, h).start()

    waiting = None
    for position, (p, block, h) in enumerate(order):

        @pl.loop(0, per_piece)
        def _(j):
            w_copy(position, j).wait()
            at = pl.ds(pl.multiple_of(block * width + h * half + j * chunk, chunk), chunk)
            part_buf[:, pl.ds(pl.multiple_of(h * half + j * chunk, chunk), chunk)] = lax.dot_general(
                cot, w_buf[at, :], (((1,), (1,)), ((), ())), preferred_element_type=jnp.float32
            )

        if position % 2 == 0:
            at = pl.ds(h * half, half)
            sib_out[p, :, at] = part_buf[:, at].astype(jnp.bfloat16)
            sib_copy(p, h).start()
            if waiting is not None:
                send_sum(*waiting)
                waiting = None
        elif position < 2 * halves * (chips - 1):
            waiting = (p, h)

    flip = jnp.where(
        lax.rem(iota((kernel_size, kernel_size), 0) + iota((kernel_size, kernel_size), 1), kernel_size) == 0, 1.0, 0.0
    ).astype(jnp.bfloat16)
    frev_buf[...] = jnp.dot(f_ref[...].astype(jnp.bfloat16), flip, preferred_element_type=jnp.float32)

    @pl.when(has_previous)
    def _():
        kv_copy.wait_recv()

    @pl.when(jnp.logical_not(has_previous))
    def _():
        rim_buf[...] = jnp.zeros_like(rim_buf)

    def own_copy(h, slot):
        at = pl.ds(h * half, half)
        return remote(gather.at[me, :, at], gather.at[slot, :, at], own_send.at[h], own_recv.at[h], wid=sibling)

    def peer_copy(p, h, slot, slot_chip):
        at = pl.ds(h * half, half)
        return remote(
            gather.at[me, :, at], gather.at[slot, :, at],
            peer_send.at[p * halves + h], peer_recv.at[slot_chip * halves + h], wid=p * 2 + core,
        )

    def fwd_copy(p, h, slot):
        at = pl.ds(h * half, half)
        return remote(
            gather.at[p * 2 + core, :, at], gather.at[slot, :, at],
            fwd_send.at[p * halves + h], fwd_recv.at[p * halves + h], wid=sibling,
        )

    for h in range(halves):

        @pl.loop(h * (half // tile), (h + 1) * (half // tile))
        def _(i):
            at = pl.ds(pl.multiple_of(i * tile, tile), tile)
            which = pl.ds(pl.multiple_of(i * tile_groups, tile_groups), tile_groups)
            extended = jnp.concatenate([rim_buf[:, at], kv_buf[:, at]], axis=0)
            conv = forward_tile(frev_buf[which, :], extended, group_size)
            conv_buf[:, at] = conv
            gather[me, :, at] = (q_ref[:, at].astype(jnp.float32) * conv).astype(jnp.bfloat16)

        for p in other_chips:
            peer_copy(p, h, me, chip).start()
        own_copy(h, me).start()

    for h in range(halves):
        sib_copy(chip, h).wait_recv()
        for p in other_chips:
            pre_copy(p, p, h).wait_recv()

    @pl.loop(0, width // tile)
    def _(i):
        at = pl.ds(pl.multiple_of(i * tile, tile), tile)
        grad_gated = part_buf[:, at] + sib_in[chip, :, at].astype(jnp.float32)
        for p in other_chips:
            grad_gated = grad_gated + pre_in[p, :, at].astype(jnp.float32)
        gc_buf[:, at] = (grad_gated * q_ref[:, at].astype(jnp.float32)).astype(jnp.bfloat16)
        gq_ref[:, at] = (grad_gated * conv_buf[:, at]).astype(jnp.bfloat16)

    gc_copy = remote(gc_buf, gcn_buf, gc_send, gc_recv, tok=lax.rem(tok + n_tok - 1, n_tok))

    @pl.when(has_previous)
    def _():
        gc_copy.start()

    @pl.loop(0, width // tile)
    def _(i):
        at = pl.ds(pl.multiple_of(i * tile, tile), tile)
        which = pl.ds(pl.multiple_of(i * tile_groups, tile_groups), tile_groups)
        extended = jnp.concatenate([rim_buf[:, at], kv_buf[:, at]], axis=0)
        local_buf[which, :] = filter_tile(extended, gc_buf[:, at], tile_groups, group_size)

    local_buf[...] = jnp.dot(
        local_buf[...], flip.astype(jnp.float32), preferred_element_type=jnp.float32, precision=lax.Precision.HIGHEST
    )

    def owned(t):
        return pl.ds(pl.multiple_of(t * rows, rows), rows)

    def term_copy(t, slot):
        return remote(local_buf.at[owned(lax.rem(t, owners))], terms_buf.at[slot], term_send.at[t], term_recv.at[slot], tok=t)

    def sum_copy(t, owner):
        return remote(all_buf.at[owned(owner)], all_buf.at[owned(owner)], sum_send.at[t], sum_recv.at[owner], tok=t)

    def if_owner(t, action):
        if owners == n_tok:
            action()
        else:
            pl.when(t < owners)(action)

    for t in other_toks:
        if_owner(t, lambda t=t: term_copy(t, tok).start())

    def project(block, start, depth, first):
        @pl.loop(0, width // chunk)
        def _(j):
            at = pl.ds(pl.multiple_of(j * chunk, chunk), chunk)
            deep = pl.ds(pl.multiple_of(block * width + start, depth), depth)
            product = jnp.dot(
                gather[block, :, pl.ds(start, depth)], w_buf[deep, at], preferred_element_type=jnp.float32
            )
            total[:, at] = product if first else total[:, at] + product

    project(me, 0, width, True)
    for h in range(halves):
        own_copy(h, sibling).wait_recv()

    def sum_terms():
        for t in other_toks:
            term_copy(t, t).wait_recv()
        terms_buf[tok] = local_buf[owned(tok), :]
        all_buf[owned(tok), :] = jnp.sum(terms_buf[...], axis=0)
        for t in other_toks:
            sum_copy(t, tok).start()

    for h in range(halves):
        for p in other_chips:
            peer_copy(p, h, p * 2 + core, p).wait_recv()
            fwd_copy(p, h, p * 2 + core).start()
    project(sibling, 0, width, False)
    for p in other_chips:
        project(p * 2 + core, 0, width, False)
    if_owner(tok, sum_terms)
    for p in other_chips:
        for h in range(halves):
            fwd_copy(p, h, p * 2 + 1 - core).wait_recv()
        project(p * 2 + 1 - core, 0, width, False)
    out_ref[...] = total[...].astype(jnp.bfloat16)

    @pl.when(has_next)
    def _():
        gc_copy.wait_recv()

    @pl.when(jnp.logical_not(has_next))
    def _():
        gcn_buf[...] = jnp.zeros_like(gcn_buf)

    own_out[...] = gc_buf[...]
    next_out[...] = gcn_buf[...]
    for t in other_toks:
        if_owner(t, lambda t=t: sum_copy(t, t).wait_recv())
    gf_ref[...] = all_buf[...]

    pl.when(has_next)(lambda: kv_copy.wait_send())
    pl.when(has_previous)(lambda: gc_copy.wait_send())
    for h in range(halves):
        for p in other_chips + [chip]:
            sib_copy(p, h).wait_send()
        for p in other_chips:
            pre_copy(p, chip, h).wait_send()
    for h in range(halves):
        own_copy(h, me).wait_send()
        for p in other_chips:
            peer_copy(p, h, me, chip).wait_send()
            fwd_copy(p, h, p * 2 + core).wait_send()
    for t in other_toks:
        if_owner(t, lambda t=t: term_copy(t, tok).wait_send())

    def sums_sent():
        for t in other_toks:
            sum_copy(t, tok).wait_send()

    if_owner(tok, sums_sent)


def last_kernel(
    group_size, tile, scale, out_ref, gq_ref, own_ref, next_ref, sums_ref, k_ref, v_ref, f_ref,
    out, gq, gk, gv, gf,
):
    out[...] = out_ref[...]
    gq[...] = gq_ref[...]
    gf[...] = sums_ref[...] * scale
    tile_groups = tile // group_size

    @pl.loop(0, k_ref.shape[1] // tile)
    def _(i):
        at = pl.ds(pl.multiple_of(i * tile, tile), tile)
        which = pl.ds(pl.multiple_of(i * tile_groups, tile_groups), tile_groups)
        grads = jnp.concatenate([own_ref[:, at], next_ref[:, at]], axis=0)
        grad_kv = backward_tile(f_ref[which, :], grads, group_size)
        gk[:, at] = (grad_kv * v_ref[:, at].astype(jnp.float32)).astype(jnp.bfloat16)
        gv[:, at] = (grad_kv * k_ref[:, at].astype(jnp.float32)).astype(jnp.bfloat16)


def local(queries, key_branch, value_branch, filters, out_weight, cotangent):
    length, width = queries.shape
    groups, kernel_size = filters.shape
    n_tok, n_wid = lax.axis_size("tok"), lax.axis_size("wid")
    chips = n_wid // 2
    group_size = width // groups
    tile, halves = min(128, width // 2), min(4, max(2, width // 128))
    chunk = min(512, width // halves)
    step = min(512, width)
    owners = min(n_tok, groups // 8)
    bf16, f32 = jnp.bfloat16, jnp.float32
    wide = jax.ShapeDtypeStruct((length, width), bf16)
    dma = pltpu.SemaphoreType.DMA
    vmem = pl.BlockSpec(memory_space=pltpu.VMEM)
    results = pl.pallas_call(
        functools.partial(kernel, (n_tok, n_wid, tile, chunk, halves, owners)),
        in_specs=[vmem] * 4 + [pl.BlockSpec(memory_space=pl.ANY), vmem],
        out_specs=[vmem] * 5,
        out_shape=[wide] * 4 + [jax.ShapeDtypeStruct(filters.shape, f32)],
        scratch_shapes=[
            pltpu.VMEM(out_weight.shape, bf16),
            pltpu.VMEM((length, width), bf16),
            pltpu.VMEM((length, width), bf16),
            pltpu.VMEM((length, width), f32),
            pltpu.VMEM((length, width), f32),
            pltpu.VMEM((chips, length, width), bf16),
            pltpu.VMEM((chips, length, width), bf16),
            pltpu.VMEM((chips, length, width), bf16),
            pltpu.VMEM((chips, length, width), bf16),
            pltpu.VMEM((n_wid, length, width), bf16),
            pltpu.VMEM((length, width), f32),
            pltpu.VMEM((length, width), bf16),
            pltpu.VMEM((length, width), bf16),
            pltpu.VMEM(filters.shape, f32),
            pltpu.VMEM(filters.shape, f32),
            pltpu.VMEM((n_tok, groups // owners, kernel_size), f32),
            pltpu.VMEM(filters.shape, f32),
            dma((n_wid * (width // chunk),)),
            dma, dma,
            dma((chips * halves,)), dma((chips * halves,)), dma((chips * halves,)), dma((chips * halves,)),
            dma((halves,)), dma((halves,)),
            dma((chips * halves,)), dma((chips * halves,)), dma((chips * halves,)), dma((chips * halves,)),
            dma, dma,
            dma((n_tok,)), dma((n_tok,)), dma((n_tok,)), dma((n_tok,)),
        ],
        compiler_params=pltpu.CompilerParams(
            collective_id=0, has_side_effects=True, vmem_limit_bytes=60 * 2**20
        ),
        cost_estimate=pl.CostEstimate(
            flops=4 * length * width * width * n_wid, bytes_accessed=2 * width * width * n_wid, transcendentals=0
        ),
    )(queries, key_branch, value_branch, filters, out_weight, cotangent)
    channels = pl.BlockSpec((length, step), lambda i: (0, i))
    by_group = pl.BlockSpec((step // group_size, kernel_size), lambda i: (i, 0))
    scale = 1.0 / math.sqrt(length * n_tok * group_size)
    return pl.pallas_call(
        functools.partial(last_kernel, group_size, tile, scale),
        grid=(width // step,),
        in_specs=[channels] * 4 + [by_group, channels, channels, by_group],
        out_specs=[channels] * 4 + [by_group],
        out_shape=[wide] * 4 + [jax.ShapeDtypeStruct(filters.shape, f32)],
    )(*results, key_branch, value_branch, filters)


def solution(mesh):
    return jax.shard_map(
        local,
        mesh=mesh,
        in_specs=(
            P("tok", "wid"),
            P("tok", "wid"),
            P("tok", "wid"),
            P("wid", None),
            P(None, "wid"),
            P("tok", "wid"),
        ),
        out_specs=(
            P("tok", "wid"),
            P("tok", "wid"),
            P("tok", "wid"),
            P("tok", "wid"),
            P("wid", None),
        ),
        check_vma=False,
    )
```
